256 devices in a mesh: dp: 32 (over x, z), mp: 8 (over y, core).
Axes of the slice: x: 4, y: 4, z: 8, core: 2. Of those that a mesh axis runs over, the one named last changes fastest.
Arguments:
- train_inputs: bfloat16 [96, 320, 27648], P('dp', None, 'mp'), may hold values from -6 to 6
- train_grads_out: bfloat16 [96, 320, 5120], P('dp', None, 'mp'), may hold values from -6 to 6
- query_inputs: bfloat16 [32, 320, 27648], P('dp', None, 'mp'), may hold values from -6 to 6
- query_grads_out: bfloat16 [32, 320, 5120], P('dp', None, 'mp'), may hold values from -6 to 6
- proj_in: bfloat16 [27648, 256], P('mp'), may hold values from -0.0390625 to 0.0390625
- proj_out: bfloat16 [5120, 256], P('mp'), may hold values from -0.078125 to 0.078125
- out_inverse: float32 [256, 256], replicated, as said below
- in_inverse: float32 [256, 256], replicated, as said below
Outputs:
- scores: float32 [32, 96], P(None, 'dp')
The draws below stay inside these ranges and needn't reach their ends.
Inputs may be any that keep to these rules, and one draw needn't show every extreme that they name: `out_inverse`: each row's diagonal entry lies between 0.5 and 4; the matrix is not symmetric. `in_inverse`: each row's diagonal entry lies between 0.5 and 4; the matrix is not symmetric.
All inputs are finite; a program needn't handle non-finite values.
Results may differ from the reference program's by a relative error of at most 0.0003.
Values sent between devices are 32-bit elements; how exact they have to be, the bound alone decides.
No kernel may reach another device: no remote copies, remote signals or barrier semaphores. Data moves between devices by JAX's collectives and lax.ppermute only.
A program may use at most 64 MiB of HBM per device.

```python
import jax
import jax.numpy as jnp
from jax import lax

D = 5120
FF = 27648
RANK = 256
LEN = 320
TRAIN = 96
QUERIES = 32


def inverse_factor(key):
    diag_key, off_key = jax.random.split(key)
    diagonal = jax.random.uniform(diag_key, (RANK,), jnp.float32, 0.5, 2.0)
    off = jax.random.normal(off_key, (RANK, RANK), jnp.float32) * RANK ** (-0.5)
    eye = jnp.eye(RANK, dtype=jnp.float32)
    return off * (1.0 - eye) + eye * diagonal[:, None]


def draw_out_inverse(key, part):
    key = jax.random.fold_in(key, 11)
    return inverse_factor(key)


def draw_in_inverse(key, part):
    key = jax.random.fold_in(key, 23)
    return inverse_factor(key)


def shard_levels(rng, shape, pieces, low, top_value):
    loudness = 1.0
    for axis_at, shards_of in pieces:
        draws = jax.random.uniform(jax.random.fold_in(jax.random.fold_in(rng, 6), axis_at), (shards_of,), jnp.float32, low / len(pieces), top_value / len(pieces))
        loudness = loudness * jnp.repeat(jnp.exp(draws), shape[axis_at] // shards_of).reshape((-1,) + (1,) * (len(shape) - 1 - axis_at))
    return loudness


def centred(key, shape, deviation, bound, cuts=(), kind=jnp.bfloat16):
    result = jax.random.normal(key, shape, jnp.float32) * deviation
    if len(cuts) > 0:
        result = shard_levels(key, shape, cuts, -0.22, 0.18) * result
    return jnp.clip(result, min=-bound, max=bound).astype(kind)


def setup_inputs(seed: int = 0) -> dict:
    key_of = jax.random.split(jax.random.key(seed), 9)
    return {
        "train_inputs": centred(key_of[0], (TRAIN, LEN, FF), 1.0, 6.0, ((0, 32), (2, 8))),
        "train_grads_out": centred(key_of[1], (TRAIN, LEN, D), 1.0, 6.0, ((0, 32), (2, 8))),
        "query_inputs": centred(key_of[2], (QUERIES, LEN, FF), 1.0, 6.0, ((0, 32), (2, 8))),
        "query_grads_out": centred(key_of[3], (QUERIES, LEN, D), 1.0, 6.0, ((0, 32), (2, 8))),
        "proj_in": centred(key_of[4], (FF, RANK), FF ** -0.5, 0.0390625, ((0, 8),)),
        "proj_out": centred(key_of[5], (D, RANK), D ** -0.5, 0.078125, ((0, 8),)),
        "out_inverse": draw_out_inverse(jax.random.fold_in(key_of[8], 71), 0),
        "in_inverse": draw_in_inverse(jax.random.fold_in(key_of[8], 71), 0),
    }


def reference(train_inputs, train_grads_out, query_inputs, query_grads_out, proj_in, proj_out, out_inverse, in_inverse):
    highest = lax.Precision.HIGHEST
    factor = LEN ** (-0.5)
    wide_in = proj_in.astype(jnp.float32)
    wide_out = proj_out.astype(jnp.float32)

    def one_grad(pair):
        acts, back = pair
        xproj = jnp.dot(acts.astype(jnp.float32), wide_in, precision=highest, preferred_element_type=jnp.float32)
        yproj = jnp.dot(back.astype(jnp.float32), wide_out, precision=highest, preferred_element_type=jnp.float32)
        return jnp.dot(yproj.T, xproj, precision=highest) * factor
    train_grad = lax.map(one_grad, (train_inputs, train_grads_out))
    query_grad = lax.map(one_grad, (query_inputs, query_grads_out))
    left = jnp.einsum('ik,qkj->qij', out_inverse, query_grad, precision=highest)
    precond = jnp.einsum('qik,kj->qij', left, in_inverse, precision=highest)
    return jnp.einsum('qij,sij->qs', precond, train_grad, precision=highest) / RANK
```

```python
import jax
import jax.numpy as jnp
from jax import lax
from jax.sharding import Mesh, PartitionSpec as P

HIGH = lax.Precision.HIGH
PAIRS_A = [(0, 1), (1, 0), (2, 3), (3, 2)]
PAIRS_B = [(0, 3), (3, 0), (1, 2), (2, 1)]
CORES = [(0, 1), (1, 0)]


def shift(value, axis, size, by):
    return lax.ppermute(value, axis, [((i + by) % size, i) for i in range(size)])


def project(acts, weights):
    return jnp.einsum("slk,kr->slr", acts, weights, preferred_element_type=jnp.float32)


def halves(value, index, axis):
    first, second = jnp.split(value, 2, axis)
    swap = index == 1
    return jnp.where(swap, second, first), jnp.where(swap, first, second)


def body(
    train_inputs,
    train_grads_out,
    query_inputs,
    query_grads_out,
    proj_in,
    proj_out,
    out_inverse,
    in_inverse,
):
    length = train_inputs.shape[1]
    width = proj_in.shape[1]
    x, z, y, core = (lax.axis_index(name) for name in ("x", "z", "y", "c"))
    row_half = ((y == 1) | (y == 2)).astype(jnp.int32)
    col_half = (y >= 2).astype(jnp.int32)

    query_y = jnp.einsum("slk,ik->sli", project(query_grads_out, proj_out), out_inverse, precision=HIGH)
    query_x = jnp.einsum("slk,kj->slj", project(query_inputs, proj_in), in_inverse, precision=HIGH)
    all_y = jnp.concatenate([query_y, project(train_grads_out, proj_out)], 0)
    all_x = jnp.concatenate([query_x, project(train_inputs, proj_in)], 0)

    keep_y, send_y = halves(all_y, core, 0)
    keep_x, send_x = halves(all_x, core, 0)
    sum_y = keep_y + lax.ppermute(send_y, "c", CORES)
    sum_x = keep_x + lax.ppermute(send_x, "c", CORES)

    keep_y, send_y = halves(sum_y, row_half, 2)
    keep_x, send_x = halves(sum_x, col_half, 2)
    half_y = keep_y + lax.ppermute(send_y, "y", PAIRS_A)
    half_x = keep_x + lax.ppermute(send_x, "y", PAIRS_B)
    half_y = half_y + lax.ppermute(half_y, "y", PAIRS_B)
    half_x = half_x + lax.ppermute(half_x, "y", PAIRS_A)

    grads = jnp.einsum("sli,slj->sij", half_y, half_x, precision=HIGH)
    keep, send = halves(grads, core, 1)
    got = lax.ppermute(send, "c", CORES)
    low = jnp.where(core == 0, keep, got)
    high = jnp.where(core == 0, got, keep)
    query, train = low[:1], jnp.concatenate([low[1:], high], 0)

    near = jnp.concatenate([query, shift(query, "z", 8, 1), shift(query, "z", 8, -1)], 0)
    up = shift(near, "z", 8, 3)
    down = shift(near[:2], "z", 8, -3)
    queries = jnp.concatenate([near, up, down], 0)
    at_z = [0, 1, -1, 3, 4, 2, -3, -2]
    trains = jnp.stack([train] + [shift(train, "x", 4, by) for by in (1, 2, 3)], 0)
    part = jnp.einsum("qij,dsij->qds", queries, trains, precision=lax.Precision.HIGHEST)

    part = jnp.stack([part[:, (i - x) % 4] for i in range(4)], 0)
    part = jnp.broadcast_to(part[:, None], (4, 8) + part.shape[1:]).reshape((32,) + part.shape[1:])
    got = lax.all_to_all(part, ("x", "y", "c"), 0, 0, tiled=True)
    scores = got.reshape(4, 8, 8, 3).sum(1)
    order = [at_z.index(d) if d in at_z else at_z.index(d - 8) for d in range(8)]
    scores = scores[:, jnp.array(order)]
    scores = jnp.roll(scores, z, 1)
    return scores.reshape(32, 3) * (1.0 / (length * width))


def solution(mesh):
    devices = Mesh(mesh.devices.reshape(4, 8, 4, 2), ("x", "z", "y", "c"))
    dp, mp = ("x", "z"), ("y", "c")
    return jax.shard_map(
        body,
        mesh=devices,
        in_specs=(
            P(dp, None, mp),
            P(dp, None, mp),
            P(dp, None, mp),
            P(dp, None, mp),
            P(mp, None),
            P(mp, None),
            P(),
            P(),
        ),
        out_specs=P(None, dp),
        check_vma=False,
    )
```

```python
import functools

import jax
import jax.numpy as jnp
from jax import lax
from jax.experimental import pallas as pl
from jax.experimental.pallas import tpu as pltpu
from jax.sharding import Mesh, PartitionSpec as P

PAIRS_A = [(0, 1), (1, 0), (2, 3), (3, 2)]
PAIRS_B = [(0, 3), (3, 0), (1, 2), (2, 1)]
CORES = [(0, 1), (1, 0)]
HALF = 128
LIMIT = 24 * 2**20
WIDE = 58 * 2**20
AT_Z = (0, 7, 2, 5, 1, 6, 3, 4)


def across(value, axis, bits):
    size = {"x": 4, "z": 8}[axis]
    return lax.ppermute(value, axis, [(i, i ^ bits) for i in range(size)])


def after(value, *others):
    return lax.optimization_barrier((value, others))[0]


def dot3(a, b, dims):
    a_high, b_high = a.astype(jnp.bfloat16), b.astype(jnp.bfloat16)
    a_low = (a - a_high.astype(jnp.float32)).astype(jnp.bfloat16)
    b_low = (b - b_high.astype(jnp.float32)).astype(jnp.bfloat16)
    dot = functools.partial(
        lax.dot_general, dimension_numbers=(dims, ((), ())), preferred_element_type=jnp.float32
    )
    return dot(a_low, b_high) + dot(a_high, b_low) + dot(a_high, b_high)


def my_halves():
    y = lax.axis_index("y")
    return jnp.where((y == 1) | (y == 2), 1, 0), jnp.where(y >= 2, 1, 0)


def project_kernel(*refs):
    (tx, ty, qx, qy, w, v, oi, ii), refs = refs[:8], refs[8:]
    (q_keep, q_send, t_keep, t_send), refs = refs[:4], refs[4:]
    x_s, y_s, w_s, v_s, oi_s, ii_s, x_acc, y_acc, sems = refs
    n, length = tx.shape[:2]
    rows = [pl.ds(s * length, length) for s in range(n + 1)]
    for_y = [(v, v_s), (oi, oi_s), (qy.at[0], y_s.at[rows[0]])]
    for_y += [(ty.at[s], y_s.at[rows[s + 1]]) for s in range(n)]
    for_x = [(w, w_s), (ii, ii_s), (qx.at[0], x_s.at[rows[0]])]
    for_x += [(tx.at[s], x_s.at[rows[s + 1]]) for s in range(n)]
    copies = [pltpu.make_async_copy(a, b, sems.at[i]) for i, (a, b) in enumerate(for_y + for_x)]
    for copy in copies:
        copy.start()
    query = pl.ds(0, length)
    for copy in copies[: len(for_y)]:
        copy.wait()
    y_acc[...] = jnp.dot(y_s[...], v_s[...], preferred_element_type=jnp.float32)
    y_acc[query] = dot3(y_acc[query], oi_s[...], ((1,), (1,)))
    for copy in copies[len(for_y) :]:
        copy.wait()
    x_acc[...] = jnp.dot(x_s[...], w_s[...], preferred_element_type=jnp.float32)
    x_acc[query] = dot3(x_acc[query], ii_s[...], ((1,), (0,)))
    part = length // 2
    core = lax.axis_index("c")
    for kind, (acc, half) in enumerate(zip((y_acc, x_acc), my_halves())):
        for j in range(2):
            place = kind + 2 * jnp.where(half == j, 1, 0)
            columns = slice(j * HALF, (j + 1) * HALF)
            for s in range(n + 1):
                keep, send, t = (q_keep, q_send, 0) if s == 0 else (t_keep, t_send, s - 1)
                mine = pl.multiple_of(s * length + core * part, part)
                other = pl.multiple_of(s * length + (1 - core) * part, part)
                keep[place, t] = acc[pl.ds(mine, part), columns]
                send[place, t] = acc[pl.ds(other, part), columns]


def project(*args):
    n, length, depth = args[0].shape
    tokens, width = (n + 1) * length, args[4].shape[1]
    outs = [jax.ShapeDtypeStruct((4, k, length // 2, HALF), jnp.float32) for k in (1, 1, n, n)]
    return pl.pallas_call(
        project_kernel,
        in_specs=[pl.BlockSpec(memory_space=pl.ANY)] * 8,
        out_specs=[pl.BlockSpec(memory_space=pltpu.VMEM)] * 4,
        out_shape=outs,
        scratch_shapes=[
            pltpu.VMEM((tokens, depth), jnp.bfloat16),
            pltpu.VMEM((tokens, args[1].shape[2]), jnp.bfloat16),
            *[pltpu.VMEM(a.shape, a.dtype) for a in args[4:]],
            pltpu.VMEM((tokens, width), jnp.float32),
            pltpu.VMEM((tokens, width), jnp.float32),
            pltpu.SemaphoreType.DMA((2 * n + 6,)),
        ],
        compiler_params=pltpu.CompilerParams(vmem_limit_bytes=WIDE),
        cost_estimate=pl.CostEstimate(
            flops=2 * tokens * (depth + args[1].shape[2]) * width,
            bytes_accessed=2 * sum(a.size for a in args),
            transcendentals=0,
        ),
    )(*args)


def grad_kernel(n, ya_ref, yb_ref, xa_ref, xb_ref, keep_ref, send_ref, grad_ref):
    core = lax.axis_index("c")
    rows = HALF // 2
    mine = pl.ds(pl.multiple_of(core * rows, rows), rows)
    other = pl.ds(pl.multiple_of((1 - core) * rows, rows), rows)
    for s in range(n):
        grad_ref[...] = dot3(ya_ref[s] + yb_ref[s], xa_ref[s] + xb_ref[s], ((0,), (0,)))
        keep_ref[s] = grad_ref[mine]
        send_ref[s] = grad_ref[other]


def gradient(ya, yb, xa, xb):
    n = ya.shape[0]
    out = jax.ShapeDtypeStruct((n, HALF // 2, HALF), jnp.float32)
    return pl.pallas_call(
        functools.partial(grad_kernel, n),
        out_shape=[out, out],
        scratch_shapes=[pltpu.VMEM((HALF, HALF), jnp.float32)],
        compiler_params=pltpu.CompilerParams(vmem_limit_bytes=LIMIT),
        cost_estimate=pl.CostEstimate(
            flops=6 * ya.size * HALF, bytes_accessed=16 * ya.size, transcendentals=0
        ),
    )(ya, yb, xa, xb)


def score_kernel(four_ref, rest_ref, t0_ref, t1_ref, t2_ref, t3_ref, out_ref):
    x, z = lax.axis_index("x"), lax.axis_index("z")
    queries = [four_ref.at[i] for i in range(4)] + [rest_ref.at[i] for i in range(4)]
    lane = lax.broadcasted_iota(jnp.int32, (1, HALF), 1)
    for d, trains in enumerate((t0_ref, t1_ref, t2_ref, t3_ref)):
        row = jnp.zeros((1, HALF), jnp.float32)
        for query, by in zip(queries, AT_Z):
            place = x * 8 + jnp.bitwise_xor(z, by)
            for s in range(3):
                total = jnp.sum((query[...] * trains[s]).reshape(-1, 8, HALF), axis=0)
                total = jnp.sum(jnp.sum(total, axis=0, keepdims=True), axis=1, keepdims=True)
                row = jnp.where(lane == place + 32 * s, total, row)
        home = pl.multiple_of(jnp.bitwise_xor(x, d) * 8, 8)
        out_ref[pl.ds(home, 8), :] = jnp.broadcast_to(row, (8, HALF))


def score(four, rest, trains):
    return pl.pallas_call(
        score_kernel,
        out_shape=jax.ShapeDtypeStruct((32, HALF), jnp.float32),
        compiler_params=pltpu.CompilerParams(vmem_limit_bytes=LIMIT),
        cost_estimate=pl.CostEstimate(flops=2 * 96 * 8192, bytes_accessed=2**20, transcendentals=0),
    )(four, rest, *trains)


def finish_kernel(scale, parts_ref, out_ref):
    total = jnp.sum(parts_ref[...], axis=0, keepdims=True) * scale
    for s in range(3):
        out_ref[s : s + 1, :] = total[:, 32 * s : 32 * s + 32]


def finish(parts, scale):
    return pl.pallas_call(
        functools.partial(finish_kernel, scale),
        out_shape=jax.ShapeDtypeStruct((3, 32), jnp.float32),
        compiler_params=pltpu.CompilerParams(vmem_limit_bytes=LIMIT),
    )(parts).T


def body(
    train_inputs,
    train_grads_out,
    query_inputs,
    query_grads_out,
    proj_in,
    proj_out,
    out_inverse,
    in_inverse,
):
    length = train_inputs.shape[1]
    width = proj_in.shape[1]

    q_keep, q_send, keep, send = project(
        train_inputs, train_grads_out, query_inputs, query_grads_out, proj_in, proj_out, out_inverse, in_inverse
    )
    got = lax.ppermute(q_send, "c", CORES)
    y_got = lax.ppermute(q_keep[0] + got[0], "y", PAIRS_A)
    x_got = lax.ppermute(q_keep[1] + got[1], "y", PAIRS_B)
    y_half = (q_keep[2] + got[2]) + y_got
    x_half = (q_keep[3] + got[3]) + x_got

    got = lax.ppermute(after(send, got), "c", CORES)
    y_away, x_away = keep[0] + got[0], keep[1] + got[1]
    y_half, x_half = after((y_half, x_half), y_away)
    y_rest = lax.ppermute(y_half, "y", PAIRS_B)
    x_rest = lax.ppermute(x_half, "y", PAIRS_A)
    y_got = lax.ppermute(y_away, "y", PAIRS_A)
    x_got = lax.ppermute(x_away, "y", PAIRS_B)

    query, query_send = gradient(y_half, y_rest, x_half, x_rest)
    y_half = (keep[2] + got[2]) + y_got
    x_half = (keep[3] + got[3]) + x_got
    query = after(query + lax.ppermute(query_send, "c", CORES), (y_half, x_half))
    y_rest = lax.ppermute(y_half, "y", PAIRS_B)
    x_rest = lax.ppermute(x_half, "y", PAIRS_A)

    two = jnp.concatenate([query, across(query, "z", 7)], 0)
    four = jnp.concatenate([two, across(two, "z", 2)], 0)
    rest = across(four, "z", 1)
    keep, send = gradient(y_half, y_rest, x_half, x_rest)
    train = keep + lax.ppermute(send, "c", CORES)
    trains = [train] + [across(train, "x", bits) for bits in (1, 2, 3)]

    parts = lax.all_to_all(score(four, rest, trains), ("x", "y", "c"), 0, 0, tiled=True)
    return finish(parts, 1.0 / (length * width))


def solution(mesh):
    devices = Mesh(mesh.devices.reshape(4, 8, 4, 2), ("x", "z", "y", "c"))
    dp, mp = ("x", "z"), ("y", "c")
    return jax.shard_map(
        body,
        mesh=devices,
        in_specs=(
            P(dp, None, mp),
            P(dp, None, mp),
            P(dp, None, mp),
            P(dp, None, mp),
            P(mp, None),
            P(mp, None),
            P(),
            P(),
        ),
        out_specs=P(None, dp),
        check_vma=False,
    )
```

```python
import functools

import jax
import jax.numpy as jnp
from jax import lax
from jax.experimental import pallas as pl
from jax.experimental.pallas import tpu as pltpu
from jax.sharding import Mesh, PartitionSpec as P

PAIRS_A = [(0, 1), (1, 0), (2, 3), (3, 2)]
PAIRS_B = [(0, 3), (3, 0), (1, 2), (2, 1)]
CORES = [(0, 1), (1, 0)]
HALF = 128
LIMIT = 24 * 2**20
WIDE = 58 * 2**20
AT_Z = (0, 7, 2, 5, 1, 6, 3, 4)


def across(value, axis, bits):
    size = {"x": 4, "z": 8}[axis]
    return lax.ppermute(value, axis, [(i, i ^ bits) for i in range(size)])


def after(value, *others):
    return lax.optimization_barrier((value, others))[0]


def dot3(a, b, dims):
    a_high, b_high = a.astype(jnp.bfloat16), b.astype(jnp.bfloat16)
    a_low = (a - a_high.astype(jnp.float32)).astype(jnp.bfloat16)
    b_low = (b - b_high.astype(jnp.float32)).astype(jnp.bfloat16)
    dot = functools.partial(
        lax.dot_general, dimension_numbers=(dims, ((), ())), preferred_element_type=jnp.float32
    )
    return dot(a_low, b_high) + dot(a_high, b_low) + dot(a_high, b_high)


def my_halves():
    y = lax.axis_index("y")
    return jnp.where((y == 1) | (y == 2), 1, 0), jnp.where(y >= 2, 1, 0)


def project_kernel(*refs):
    (tx, ty, qx, qy, w, v, oi, ii), refs = refs[:8], refs[8:]
    (q_keep, q_send, t_keep, t_send), refs = refs[:4], refs[4:]
    x_s, y_s, w_s, v_s, oi_s, ii_s, x_acc, y_acc, sems = refs
    n, length = tx.shape[:2]
    rows = [pl.ds(s * length, length) for s in range(n + 1)]
    for_y = [(v, v_s), (oi, oi_s), (qy.at[0], y_s.at[rows[0]])]
    for_y += [(ty.at[s], y_s.at[rows[s + 1]]) for s in range(n)]
    for_x = [(w, w_s), (ii, ii_s), (qx.at[0], x_s.at[rows[0]])]
    for_x += [(tx.at[s], x_s.at[rows[s + 1]]) for s in range(n)]
    copies = [pltpu.make_async_copy(a, b, sems.at[i]) for i, (a, b) in enumerate(for_y + for_x)]
    for copy in copies:
        copy.start()
    query = pl.ds(0, length)
    for copy in copies[: len(for_y)]:
        copy.wait()
    y_acc[...] = jnp.dot(y_s[...], v_s[...], preferred_element_type=jnp.float32)
    y_acc[query] = dot3(y_acc[query], oi_s[...], ((1,), (1,)))
    for copy in copies[len(for_y) :]:
        copy.wait()
    x_acc[...] = jnp.dot(x_s[...], w_s[...], preferred_element_type=jnp.float32)
    x_acc[query] = dot3(x_acc[query], ii_s[...], ((1,), (0,)))
    part = length // 2
    core = lax.axis_index("c")
    for kind, (acc, half) in enumerate(zip((y_acc, x_acc), my_halves())):
        for j in range(2):
            place = kind + 2 * jnp.where(half == j, 1, 0)
            columns = slice(j * HALF, (j + 1) * HALF)
            for s in range(n + 1):
                keep, send, t = (q_keep, q_send, 0) if s == 0 else (t_keep, t_send, s - 1)
                mine = pl.multiple_of(s * length + core * part, part)
                other = pl.multiple_of(s * length + (1 - core) * part, part)
                keep[place, t] = acc[pl.ds(mine, part), columns]
                send[place, t] = acc[pl.ds(other, part), columns]


def project(*args):
    n, length, depth = args[0].shape
    tokens, width = (n + 1) * length, args[4].shape[1]
    outs = [jax.ShapeDtypeStruct((4, k, length // 2, HALF), jnp.float32) for k in (1, 1, n, n)]
    return pl.pallas_call(
        project_kernel,
        in_specs=[pl.BlockSpec(memory_space=pl.ANY)] * 8,
        out_specs=[pl.BlockSpec(memory_space=pltpu.VMEM)] * 4,
        out_shape=outs,
        scratch_shapes=[
            pltpu.VMEM((tokens, depth), jnp.bfloat16),
            pltpu.VMEM((tokens, args[1].shape[2]), jnp.bfloat16),
            *[pltpu.VMEM(a.shape, a.dtype) for a in args[4:]],
            pltpu.VMEM((tokens, width), jnp.float32),
            pltpu.VMEM((tokens, width), jnp.float32),
            pltpu.SemaphoreType.DMA((2 * n + 6,)),
        ],
        compiler_params=pltpu.CompilerParams(vmem_limit_bytes=WIDE),
        cost_estimate=pl.CostEstimate(
            flops=2 * tokens * (depth + args[1].shape[2]) * width,
            bytes_accessed=2 * sum(a.size for a in args),
            transcendentals=0,
        ),
    )(*args)


def grad_kernel(n, ya_ref, yb_ref, xa_ref, xb_ref, keep_ref, send_ref, grad_ref):
    core = lax.axis_index("c")
    rows = HALF // 2
    mine = pl.ds(pl.multiple_of(core * rows, rows), rows)
    other = pl.ds(pl.multiple_of((1 - core) * rows, rows), rows)
    for s in range(n):
        grad_ref[...] = dot3(ya_ref[s] + yb_ref[s], xa_ref[s] + xb_ref[s], ((0,), (0,)))
        keep_ref[s] = grad_ref[mine]
        send_ref[s] = grad_ref[other]


def gradient(ya, yb, xa, xb):
    n = ya.shape[0]
    out = jax.ShapeDtypeStruct((n, HALF // 2, HALF), jnp.float32)
    return pl.pallas_call(
        functools.partial(grad_kernel, n),
        out_shape=[out, out],
        scratch_shapes=[pltpu.VMEM((HALF, HALF), jnp.float32)],
        compiler_params=pltpu.CompilerParams(vmem_limit_bytes=LIMIT),
        cost_estimate=pl.CostEstimate(
            flops=6 * ya.size * HALF, bytes_accessed=16 * ya.size, transcendentals=0
        ),
    )(ya, yb, xa, xb)


def score_kernel(*refs):
    pairs, trains_of, out_ref = refs[:4], refs[4:8], refs[8]
    x, z = lax.axis_index("x"), lax.axis_index("z")
    queries = [pair.at[i] for pair in pairs for i in range(2)]
    lane = lax.broadcasted_iota(jnp.int32, (1, HALF), 1)
    for d, trains in enumerate(trains_of):
        row = jnp.zeros((1, HALF), jnp.float32)
        for query, by in zip(queries, AT_Z):
            place = x * 8 + jnp.bitwise_xor(z, by)
            for s in range(3):
                total = jnp.sum((query[...] * trains[s]).reshape(-1, 8, HALF), axis=0)
                total = jnp.sum(jnp.sum(total, axis=0, keepdims=True), axis=1, keepdims=True)
                row = jnp.where(lane == place + 32 * s, total, row)
        home = pl.multiple_of(jnp.bitwise_xor(x, d) * 8, 8)
        out_ref[pl.ds(home, 8), :] = jnp.broadcast_to(row, (8, HALF))


def score(queries, trains):
    return pl.pallas_call(
        score_kernel,
        out_shape=jax.ShapeDtypeStruct((32, HALF), jnp.float32),
        compiler_params=pltpu.CompilerParams(vmem_limit_bytes=LIMIT),
        cost_estimate=pl.CostEstimate(flops=2 * 96 * 8192, bytes_accessed=2**20, transcendentals=0),
    )(*queries, *trains)


def finish_kernel(scale, parts_ref, out_ref):
    total = jnp.sum(parts_ref[...], axis=0, keepdims=True) * scale
    for s in range(3):
        out_ref[s : s + 1, :] = total[:, 32 * s : 32 * s + 32]


def finish(parts, scale):
    return pl.pallas_call(
        functools.partial(finish_kernel, scale),
        out_shape=jax.ShapeDtypeStruct((3, 32), jnp.float32),
        compiler_params=pltpu.CompilerParams(vmem_limit_bytes=LIMIT),
    )(parts).T


def body(
    train_inputs,
    train_grads_out,
    query_inputs,
    query_grads_out,
    proj_in,
    proj_out,
    out_inverse,
    in_inverse,
):
    length = train_inputs.shape[1]
    width = proj_in.shape[1]

    q_keep, q_send, keep, send = project(
        train_inputs, train_grads_out, query_inputs, query_grads_out, proj_in, proj_out, out_inverse, in_inverse
    )
    got = lax.ppermute(q_send, "c", CORES)
    y_got = lax.ppermute(q_keep[0] + got[0], "y", PAIRS_A)
    x_got = lax.ppermute(q_keep[1] + got[1], "y", PAIRS_B)
    y_half = (q_keep[2] + got[2]) + y_got
    x_half = (q_keep[3] + got[3]) + x_got

    got = lax.ppermute(after(send, got), "c", CORES)
    y_away, x_away = keep[0] + got[0], keep[1] + got[1]
    y_half, x_half = after((y_half, x_half), y_away)
    y_rest = lax.ppermute(y_half, "y", PAIRS_B)
    x_rest = lax.ppermute(x_half, "y", PAIRS_A)
    y_got = lax.ppermute(y_away, "y", PAIRS_A)
    x_got = lax.ppermute(x_away, "y", PAIRS_B)

    query, query_send = gradient(y_half, y_rest, x_half, x_rest)
    y_half = (keep[2] + got[2]) + y_got
    x_half = (keep[3] + got[3]) + x_got
    query = after(query + lax.ppermute(query_send, "c", CORES), (y_half, x_half))
    y_rest = lax.ppermute(y_half, "y", PAIRS_B)
    x_rest = lax.ppermute(x_half, "y", PAIRS_A)

    two = jnp.concatenate([query, across(query, "z", 7)], 0)
    more = across(two, "z", 2)
    keep, send = gradient(y_half, after(y_rest, two), x_half, x_rest)
    train = keep + lax.ppermute(send, "c", CORES)
    trains = [train] + [across(train, "x", bits) for bits in (1, 2, 3)]
    queries = [two, more, across(after(two, more), "z", 1), across(more, "z", 1)]

    parts = lax.all_to_all(score(queries, trains), ("x", "y", "c"), 0, 0, tiled=True)
    return finish(parts, 1.0 / (length * width))


def solution(mesh):
    devices = Mesh(mesh.devices.reshape(4, 8, 4, 2), ("x", "z", "y", "c"))
    dp, mp = ("x", "z"), ("y", "c")
    return jax.shard_map(
        body,
        mesh=devices,
        in_specs=(
            P(dp, None, mp),
            P(dp, None, mp),
            P(dp, None, mp),
            P(dp, None, mp),
            P(mp, None),
            P(mp, None),
            P(),
            P(),
        ),
        out_specs=P(None, dp),
        check_vma=False,
    )
```

```python
import functools

import jax
import jax.numpy as jnp
from jax import lax
from jax.experimental import pallas as pl
from jax.experimental.pallas import tpu as pltpu
from jax.sharding import Mesh, PartitionSpec as P

PAIRS_A = [(0, 1), (1, 0), (2, 3), (3, 2)]
PAIRS_B = [(0, 3), (3, 0), (1, 2), (2, 1)]
CORES = [(0, 1), (1, 0)]
HALF = 128
LIMIT = 24 * 2**20
WIDE = 56 * 2**20
AT_Z = (0, 7, 2, 5, 1, 6, 3, 4)


def across(value, axis, bits):
    size = {"x": 4, "z": 8}[axis]
    return lax.ppermute(value, axis, [(i, i ^ bits) for i in range(size)])


def after(value, *others):
    return lax.optimization_barrier((value, others))[0]


def dot3(a, b, dims):
    a_high, b_high = a.astype(jnp.bfloat16), b.astype(jnp.bfloat16)
    a_low = (a - a_high.astype(jnp.float32)).astype(jnp.bfloat16)
    b_low = (b - b_high.astype(jnp.float32)).astype(jnp.bfloat16)
    dot = functools.partial(
        lax.dot_general, dimension_numbers=(dims, ((), ())), preferred_element_type=jnp.float32
    )
    return dot(a_low, b_high) + dot(a_high, b_low) + dot(a_high, b_high)


def my_halves():
    y = lax.axis_index("y")
    return jnp.where((y == 1) | (y == 2), 1, 0), jnp.where(y >= 2, 1, 0)


def project_kernel(*refs):
    (tx, ty, qx, qy, w, v, oi, ii), refs = refs[:8], refs[8:]
    (q_keep, q_send, t_keep, t_send), refs = refs[:4], refs[4:]
    x_s, y_s, w_s, v_s, oi_s, ii_s, x_acc, y_acc, sems = refs
    n, length = tx.shape[:2]
    rows = [pl.ds(s * length, length) for s in range(n + 1)]
    for_y = [(v, v_s), (oi, oi_s), (qy.at[0], y_s.at[rows[0]])]
    for_y += [(ty.at[s], y_s.at[rows[s + 1]]) for s in range(n)]
    for_x = [(w, w_s), (ii, ii_s), (qx.at[0], x_s.at[rows[0]])]
    for_x += [(tx.at[s], x_s.at[rows[s + 1]]) for s in range(n)]
    copies = [pltpu.make_async_copy(a, b, sems.at[i]) for i, (a, b) in enumerate(for_y + for_x)]
    for copy in copies:
        copy.start()
    query = pl.ds(0, length)
    for copy in copies[: len(for_y)]:
        copy.wait()
    y_acc[...] = jnp.dot(y_s[...], v_s[...], preferred_element_type=jnp.float32)
    y_acc[query] = dot3(y_acc[query], oi_s[...], ((1,), (1,)))
    for copy in copies[len(for_y) :]:
        copy.wait()
    x_acc[...] = jnp.dot(x_s[...], w_s[...], preferred_element_type=jnp.float32)
    x_acc[query] = dot3(x_acc[query], ii_s[...], ((1,), (0,)))
    part = length // 2
    core = lax.axis_index("c")
    for kind, (acc, half) in enumerate(zip((y_acc, x_acc), my_halves())):
        for j in range(2):
            place = kind + 2 * jnp.where(half == j, 1, 0)
            columns = slice(j * HALF, (j + 1) * HALF)
            for s in range(n + 1):
                keep, send, t = (q_keep, q_send, 0) if s == 0 else (t_keep, t_send, s - 1)
                mine = pl.multiple_of(s * length + core * part, part)
                other = pl.multiple_of(s * length + (1 - core) * part, part)
                keep[place, t] = acc[pl.ds(mine, part), columns]
                send[place, t] = acc[pl.ds(other, part), columns]


def project(*args):
    n, length, depth = args[0].shape
    tokens, width = (n + 1) * length, args[4].shape[1]
    outs = [pltpu.VMEM((4, k, length // 2, HALF), jnp.float32) for k in (1, 1, n, n)]
    return pl.pallas_call(
        project_kernel,
        in_specs=[pl.BlockSpec(memory_space=pl.ANY)] * 8,
        out_specs=[pl.BlockSpec(memory_space=pltpu.VMEM)] * 4,
        out_shape=outs,
        scratch_shapes=[
            pltpu.VMEM((tokens, depth), jnp.bfloat16),
            pltpu.VMEM((tokens, args[1].shape[2]), jnp.bfloat16),
            *[pltpu.VMEM(a.shape, a.dtype) for a in args[4:]],
            pltpu.VMEM((tokens, width), jnp.float32),
            pltpu.VMEM((tokens, width), jnp.float32),
            pltpu.SemaphoreType.DMA((2 * n + 6,)),
        ],
        compiler_params=pltpu.CompilerParams(vmem_limit_bytes=WIDE),
        cost_estimate=pl.CostEstimate(
            flops=2 * tokens * (depth + args[1].shape[2]) * width,
            bytes_accessed=2 * sum(a.size for a in args),
            transcendentals=0,
        ),
    )(*args)


def grad_kernel(n, ya_ref, yb_ref, xa_ref, xb_ref, keep_ref, send_ref, grad_ref):
    core = lax.axis_index("c")
    rows = HALF // 2
    mine = pl.ds(pl.multiple_of(core * rows, rows), rows)
    other = pl.ds(pl.multiple_of((1 - core) * rows, rows), rows)
    for s in range(n):
        grad_ref[...] = dot3(ya_ref[s] + yb_ref[s], xa_ref[s] + xb_ref[s], ((0,), (0,)))
        keep_ref[s] = grad_ref[mine]
        send_ref[s] = grad_ref[other]


def gradient(ya, yb, xa, xb):
    n = ya.shape[0]
    out = jax.ShapeDtypeStruct((n, HALF // 2, HALF), jnp.float32)
    return pl.pallas_call(
        functools.partial(grad_kernel, n),
        out_shape=[out, out],
        scratch_shapes=[pltpu.VMEM((HALF, HALF), jnp.float32)],
        compiler_params=pltpu.CompilerParams(vmem_limit_bytes=LIMIT),
        cost_estimate=pl.CostEstimate(
            flops=6 * ya.size * HALF, bytes_accessed=16 * ya.size, transcendentals=0
        ),
    )(ya, yb, xa, xb)


def score_kernel(*refs):
    pairs, trains_of, out_ref = refs[:4], refs[4:8], refs[8]
    x, z = lax.axis_index("x"), lax.axis_index("z")
    queries = [pair.at[i] for pair in pairs for i in range(2)]
    lane = lax.broadcasted_iota(jnp.int32, (1, HALF), 1)
    for d, trains in enumerate(trains_of):
        row = jnp.zeros((1, HALF), jnp.float32)
        for query, by in zip(queries, AT_Z):
            place = x * 8 + jnp.bitwise_xor(z, by)
            for s in range(3):
                total = jnp.sum((query[...] * trains[s]).reshape(-1, 8, HALF), axis=0)
                total = jnp.sum(jnp.sum(total, axis=0, keepdims=True), axis=1, keepdims=True)
                row = jnp.where(lane == place + 32 * s, total, row)
        home = pl.multiple_of(jnp.bitwise_xor(x, d) * 8, 8)
        out_ref[pl.ds(home, 8), :] = jnp.broadcast_to(row, (8, HALF))


def score(queries, trains):
    return pl.pallas_call(
        score_kernel,
        out_shape=jax.ShapeDtypeStruct((32, HALF), jnp.float32),
        compiler_params=pltpu.CompilerParams(vmem_limit_bytes=LIMIT),
        cost_estimate=pl.CostEstimate(flops=2 * 96 * 8192, bytes_accessed=2**20, transcendentals=0),
    )(*queries, *trains)


def finish_kernel(scale, parts_ref, out_ref):
    total = jnp.sum(parts_ref[...], axis=0, keepdims=True) * scale
    for s in range(3):
        out_ref[s : s + 1, :] = total[:, 32 * s : 32 * s + 32]


def finish(parts, scale):
    return pl.pallas_call(
        functools.partial(finish_kernel, scale),
        out_shape=jax.ShapeDtypeStruct((3, 32), jnp.float32),
        compiler_params=pltpu.CompilerParams(vmem_limit_bytes=LIMIT),
    )(parts).T


def body(
    train_inputs,
    train_grads_out,
    query_inputs,
    query_grads_out,
    proj_in,
    proj_out,
    out_inverse,
    in_inverse,
):
    length = train_inputs.shape[1]
    width = proj_in.shape[1]

    q_keep, q_send, keep, send = project(
        train_inputs, train_grads_out, query_inputs, query_grads_out, proj_in, proj_out, out_inverse, in_inverse
    )
    got = lax.ppermute(q_send, "c", CORES)
    y_got = lax.ppermute(q_keep[0] + got[0], "y", PAIRS_A)
    x_got = lax.ppermute(q_keep[1] + got[1], "y", PAIRS_B)
    y_half = (q_keep[2] + got[2]) + y_got
    x_half = (q_keep[3] + got[3]) + x_got

    got = lax.ppermute(after(send, got), "c", CORES)
    y_away, x_away = keep[0] + got[0], keep[1] + got[1]
    y_half, x_half = after((y_half, x_half), y_away)
    y_rest = lax.ppermute(y_half, "y", PAIRS_B)
    x_rest = lax.ppermute(x_half, "y", PAIRS_A)
    y_got = lax.ppermute(y_away, "y", PAIRS_A)
    x_got = lax.ppermute(x_away, "y", PAIRS_B)

    query, query_send = gradient(y_half, y_rest, x_half, x_rest)
    y_half = (keep[2] + got[2]) + y_got
    x_half = (keep[3] + got[3]) + x_got
    query = after(query + lax.ppermute(query_send, "c", CORES), (y_half, x_half))
    y_rest = lax.ppermute(y_half, "y", PAIRS_B)
    x_rest = lax.ppermute(x_half, "y", PAIRS_A)

    two = jnp.concatenate([query, across(query, "z", 7)], 0)
    more = across(two, "z", 2)
    keep, send = gradient(y_half, after(y_rest, two), x_half, x_rest)
    train = keep + lax.ppermute(send, "c", CORES)
    trains = [train] + [across(train, "x", bits) for bits in (1, 2, 3)]
    queries = [two, more, across(after(two, more), "z", 1), across(more, "z", 1)]

    parts = lax.all_to_all(score(queries, trains), ("x", "y", "c"), 0, 0, tiled=True)
    return finish(parts, 1.0 / (length * width))


def solution(mesh):
    devices = Mesh(mesh.devices.reshape(4, 8, 4, 2), ("x", "z", "y", "c"))
    dp, mp = ("x", "z"), ("y", "c")
    return jax.shard_map(
        body,
        mesh=devices,
        in_specs=(
            P(dp, None, mp),
            P(dp, None, mp),
            P(dp, None, mp),
            P(dp, None, mp),
            P(mp, None),
            P(mp, None),
            P(),
            P(),
        ),
        out_specs=P(None, dp),
        check_vma=False,
    )
```
